32 devices in a mesh: row: 4 (over y, core), col: 8 (over z, x).
Axes of the slice: x: 2, y: 2, z: 4, core: 2. Of those that a mesh axis runs over, the one named last changes fastest.
Arguments:
- points: bfloat16 [65536, 512], P(('row', 'col')), may hold values from -6 to 6
- targets: float32 [65536, 256], P(('row', 'col'))
- plan: int32 [6], replicated, may hold values from 0 to 127
- block_inverse: float32 [6, 512, 512], replicated
Outputs:
- residual: float32 [65536, 256], P(('row', 'col'))
- block_steps: bfloat16 [6, 512, 256], replicated
- losses: float32 [6], replicated
The draws below stay inside these ranges and needn't reach their ends.
All inputs are finite; a program needn't handle non-finite values.
Results may differ from the reference program's by a relative error of at most 0.0062.
Values may be sent and summed in bfloat16 or wider, within the bound.
No kernel may reach another device: no remote copies, remote signals or barrier semaphores. Data moves between devices by JAX's collectives and lax.ppermute only.
A program may use at most 64 MiB of HBM per device.

```python
import jax
import jax.numpy as jnp
from jax import lax

F = 512
K = 256
BLK = 512
ROUNDS = 6
N = 65536
NB = 128


def draw_targets(key, part):
    first, second = jax.random.split(key, 2)
    position = jnp.arange(N, dtype=jnp.float32) / max(N - 1, 1)
    rough = jax.random.uniform(second, (N, 1), jnp.float32, 0.5, 1.5)
    base = jax.random.normal(first, (N, K), jnp.float32)
    scale = jnp.power(3.0, 0.5 * position)
    return base * rough * scale[:, None]


def draw_block_inverse(key, part):
    first, second = jax.random.split(key)
    diagonal = jax.random.uniform(first, (ROUNDS, BLK), jnp.float32, 0.15, 0.45)
    centre = -0.28 / BLK
    off = jax.random.normal(second, (ROUNDS, BLK, BLK), jnp.float32) * (0.15 / BLK ** 0.5) + centre
    eye = jnp.eye(BLK, dtype=jnp.float32)
    return off * (1.0 - eye)[None] + diagonal[:, :, None] * eye[None]


def place_ends(drawn, key, least, high):
    spot = [jax.random.randint(jax.random.fold_in(key, axis), (), 0, length) for axis, length in enumerate(drawn.shape)]
    widest = drawn.shape.index(max(drawn.shape))
    neighbour = spot[:widest] + [(spot[widest] + 1) % drawn.shape[widest]] + spot[widest + 1:]
    return drawn.at[tuple(spot)].set(least).at[tuple(neighbour)].set(high)


def block_levels(stream_key, dims, cuts, least, high):
    factor_of = 1.0
    for dim, parts in cuts:
        steps = jax.random.uniform(jax.random.fold_in(jax.random.fold_in(stream_key, 6), dim), (parts,), jnp.float32, least / len(cuts), high / len(cuts))
        factor_of = factor_of * jnp.repeat(jnp.exp(steps), dims[dim] // parts).reshape((-1,) + (1,) * (len(dims) - 1 - dim))
    return factor_of


def bell_draw(stream_key, shape, width, most, cuts=(), kind=jnp.bfloat16):
    array = jax.random.normal(stream_key, shape, jnp.float32) * width
    if len(cuts) > 0:
        array = block_levels(stream_key, shape, cuts, -0.22, 0.18) * array
    return jnp.clip(array, min=-most, max=most).astype(kind)


def setup_inputs(seed: int = 0) -> dict:
    key_list = jax.random.split(jax.random.key(seed), 5)
    points = bell_draw(key_list[0], (N, F), 1.0, 6.0, ((0, 32),))
    targets = draw_targets(jax.random.fold_in(key_list[4], 71), 0)
    plan = place_ends(jax.random.randint(key_list[2], (ROUNDS,), 0, NB), jax.random.fold_in(key_list[2], 1), 0, NB - 1).astype(jnp.int32)
    block_inverse = draw_block_inverse(jax.random.fold_in(key_list[4], 71), 0)
    return dict(points=points, targets=targets, plan=plan, block_inverse=block_inverse)


RIDGE = 1.0


def reference(points, targets, plan, block_inverse):
    gamma = 2.0 / F
    sqnorm = jnp.sum(jnp.square(points.astype(jnp.float32)), axis=1)
    residual = targets
    group = min(N, 8192)
    losses = []
    updates = []
    for r in range(ROUNDS):
        start = (plan[r] * BLK).astype(jnp.int32)
        block_rows = lax.dynamic_slice_in_dim(residual, start, BLK, 0)
        step = jnp.dot(block_inverse[r], block_rows, precision=lax.Precision.HIGHEST)
        step_half = step.astype(jnp.bfloat16)
        block_points = lax.dynamic_slice_in_dim(points, start, BLK, 0)
        block_norm = lax.dynamic_slice_in_dim(sqnorm, start, BLK, 0)

        def update(args):
            pts, norms, res = args
            inner = lax.dot_general(pts, block_points, (((1,), (1,)), ((), ())), preferred_element_type=jnp.float32)
            kernel = jnp.exp(-gamma * (norms[:, None] + block_norm[None, :] - 2.0 * inner)).astype(jnp.bfloat16)
            return res - jnp.dot(kernel, step_half, preferred_element_type=jnp.float32)

        residual = lax.map(update, (points.reshape(N // group, group, F), sqnorm.reshape(N // group, group), residual.reshape(N // group, group, K))).reshape(N, K)
        block_rows = lax.dynamic_slice_in_dim(residual, start, BLK, 0)
        residual = lax.dynamic_update_slice_in_dim(residual, block_rows - RIDGE * step, start, 0)
        updates.append(step_half)
        losses.append(jnp.sum(residual * residual) / (N * K))
    return residual, jnp.stack(updates), jnp.stack(losses).astype(jnp.float32)
```

```python
import functools
import math

import jax
import jax.numpy as jnp
from jax import lax
from jax.experimental import pallas as pl
from jax.experimental.pallas import tpu as pltpu
from jax.sharding import PartitionSpec as P

RIDGE = 1.0
AXES = ("row", "col")
HALVINGS = 3
NT = (((1,), (1,)), ((), ()))
LOG2E = math.log2(math.e)
MIB = 1 << 20


def stage_bits(mesh_shape):
    cols = mesh_shape["col"].bit_length() - 1
    rows = mesh_shape["row"].bit_length() - 1
    core = cols
    along_col = list(range(cols))
    along_row = list(range(cols + 1, cols + rows))
    rest = along_col[2:] + along_row[1:]
    first = along_col[:2] + along_row[:1] + rest
    second = along_row[:1] + along_col[:2] + rest
    return core, (first, second)


def swap(x, devices, bit_of):
    return lax.ppermute(x, AXES, [(i, i ^ (1 << bit_of(i))) for i in range(devices)])


class Route:
    def __init__(self, mesh_shape):
        self.devices = mesh_shape["row"] * mesh_shape["col"]
        self.core, self.orders = stage_bits(mesh_shape)
        self.stages = len(self.orders[0])
        self.halvings = min(HALVINGS, self.stages)
        self.here = lax.axis_index("row") * mesh_shape["col"] + lax.axis_index("col")
        self.side = (self.here >> self.core) & 1

    def swap_core(self, x):
        return swap(x, self.devices, lambda i: self.core)

    def swap_stage(self, x, k):
        return swap(x, self.devices, lambda i: self.orders[(i >> self.core) & 1][k])

    def bit(self, index, k, side=None):
        side = self.side if side is None else side
        first, second = self.orders
        return jnp.where(side == 0, (index >> first[k]) & 1, (index >> second[k]) & 1)

    def piece_rows(self, blocksize):
        count = 1 << self.halvings
        pieces = []
        for side in (self.side, 1 - self.side):
            for p in range(count):
                row = side * (blocksize // 2)
                for k in range(self.halvings):
                    flipped = self.bit(self.here, k, side) ^ ((p >> (self.halvings - 1 - k)) & 1)
                    row = row + flipped * (blocksize >> (k + 2))
                pieces.append(row)
        return jnp.stack(pieces).astype(jnp.int32)

    def spread(self, send, keep, owner):
        recv = self.swap_core(send)
        mine = keep
        same = ((owner >> self.core) & 1) == self.side
        for k in range(self.halvings):
            bit = self.bit(self.here, k)
            rows = mine.shape[1] // 2

            def half(which):
                return jnp.where(
                    same[:, None, None],
                    lax.dynamic_slice_in_dim(mine, which * rows, rows, 1),
                    lax.dynamic_slice_in_dim(recv, which * rows, rows, 1),
                )

            going, staying = half(1 - bit), half(bit)
            recv = self.swap_stage(going, k)
            mine = staying
            same = self.bit(owner, k) == bit
        for k in range(self.halvings, self.stages):
            mine = jnp.where(same[:, None, None], mine, recv)
            recv = self.swap_stage(mine, k)
            same = self.bit(owner, k) == self.bit(self.here, k)
        mine = jnp.where(same[:, None, None], mine, recv)[None]
        for k in reversed(range(self.halvings)):
            mine = jnp.concatenate([mine, self.swap_stage(mine, k)], 0)
        return mine, self.swap_core(mine)

    def total(self, x):
        x = x + self.swap_core(x)
        for k in range(self.stages):
            x = x + swap(x, self.devices, lambda i: self.orders[0][k])
        return x


def pick_kernel(going_ref, staying_ref, src_a, src_b, out_a, out_b):
    out_a[0] = src_a[...].astype(out_a.dtype)
    out_b[0] = src_b[...].astype(out_b.dtype)


def pick(array, going, staying, half):
    slots = going.shape[0]
    width = array.shape[1]
    shape = jax.ShapeDtypeStruct((slots, half, width), jnp.bfloat16)
    out = pl.BlockSpec((1, half, width), lambda r, a, b: (r, 0, 0))
    return pl.pallas_call(
        pick_kernel,
        out_shape=(shape, shape),
        grid_spec=pltpu.PrefetchScalarGridSpec(
            num_scalar_prefetch=2,
            grid=(slots,),
            in_specs=[
                pl.BlockSpec((half, width), lambda r, a, b: (a[r], 0)),
                pl.BlockSpec((half, width), lambda r, a, b: (b[r], 0)),
            ],
            out_specs=(out, out),
        ),
        name="pick",
    )(going, staying, array, array)


def squares(p):
    wide = p.astype(jnp.float32)
    wide = wide * wide
    high = wide.astype(jnp.bfloat16)
    return high, (wide - high.astype(jnp.float32)).astype(jnp.bfloat16)


def column_norms(p, scale):
    high, low = squares(p)
    ones = jnp.ones((p.shape[1], 128), jnp.bfloat16)
    both = jnp.dot(high, ones, preferred_element_type=jnp.float32)
    return scale * (both + jnp.dot(low, ones, preferred_element_type=jnp.float32))


def row_norms(p, scale):
    high, low = squares(p)
    ones = jnp.ones((8, p.shape[1]), jnp.bfloat16)
    both = lax.dot_general(ones, high, NT, preferred_element_type=jnp.float32)
    return scale * (both + lax.dot_general(ones, low, NT, preferred_element_type=jnp.float32))


def prepare_kernel(scale, points, inverse, norms, high, low):
    norms[...] = column_norms(points[...], scale)
    b = inverse[0]
    top = b.astype(jnp.bfloat16)
    high[0] = top
    low[0] = (b - top.astype(jnp.float32)).astype(jnp.bfloat16)


def prepare(points, inverse, scale):
    rounds, size, _ = inverse.shape
    rows, features = points.shape
    tile = rows // 4
    last = rows // tile - 1
    terms = jax.ShapeDtypeStruct(inverse.shape, jnp.bfloat16)
    block = pl.BlockSpec((1, size, size), lambda r: (r, 0, 0))
    return pl.pallas_call(
        functools.partial(prepare_kernel, scale),
        out_shape=(jax.ShapeDtypeStruct((rows, 128), jnp.float32), terms, terms),
        grid=(rounds,),
        in_specs=[
            pl.BlockSpec((tile, features), lambda r: (jnp.minimum(r, last), 0)),
            block,
        ],
        out_specs=(pl.BlockSpec((tile, 128), lambda r: (jnp.minimum(r, last), 0)), block, block),
        cost_estimate=pl.CostEstimate(flops=0, bytes_accessed=16 * MIB, transcendentals=0),
        name="prepare",
    )(points, inverse)


def assemble_kernel(scale, rows_ref, mine, other, out, across, down):
    count = mine.shape[0]
    piece = mine.shape[2]
    for p in range(count):
        out[0, pl.ds(pl.multiple_of(rows_ref[p], piece), piece), :] = mine[p, 0]
        out[0, pl.ds(pl.multiple_of(rows_ref[count + p], piece), piece), :] = other[p, 0]
    block = out[0]
    across[0] = row_norms(block, scale)
    down[0] = column_norms(block, scale)


def assemble(mine, other, piece_rows, scale):
    count, slots, piece, width = mine.shape
    size = 2 * count * piece
    src = pl.BlockSpec((count, 1, piece, width), lambda r, _: (0, r, 0, 0))

    def dst(*shape):
        return pl.BlockSpec((1,) + shape, lambda r, _: (r, 0, 0))

    return pl.pallas_call(
        functools.partial(assemble_kernel, scale),
        out_shape=(
            jax.ShapeDtypeStruct((slots, size, width), jnp.bfloat16),
            jax.ShapeDtypeStruct((slots, 8, size), jnp.float32),
            jax.ShapeDtypeStruct((slots, size, 128), jnp.float32),
        ),
        grid_spec=pltpu.PrefetchScalarGridSpec(
            num_scalar_prefetch=1,
            grid=(slots,),
            in_specs=[src, src],
            out_specs=(dst(size, width), dst(8, size), dst(size, 128)),
        ),
        cost_estimate=pl.CostEstimate(flops=0, bytes_accessed=12 * MIB, transcendentals=0),
        name="assemble",
    )(piece_rows, mine, other)


def gram_kernel(scale, left_ids, right_ids, left, right, down, across, out):
    inner = lax.dot_general(left[0], right[0], NT, preferred_element_type=jnp.float32)
    width = out.shape[2]
    offset = jnp.concatenate([down[0]] * (width // 128), axis=1) + across[0, 0:1, :]
    out[0] = jnp.exp2(inner * scale + offset).astype(out.dtype)


def gram(left, right, down, across, pairs, scale):
    size, features = left.shape[1:]
    width = right.shape[1]
    left_ids = jnp.array([i for i, _ in pairs], jnp.int32)
    right_ids = jnp.array([j for _, j in pairs], jnp.int32)
    n = len(pairs)
    return pl.pallas_call(
        functools.partial(gram_kernel, scale),
        out_shape=jax.ShapeDtypeStruct((n, size, width), jnp.bfloat16),
        grid_spec=pltpu.PrefetchScalarGridSpec(
            num_scalar_prefetch=2,
            grid=(n,),
            in_specs=[
                pl.BlockSpec((1, size, features), lambda g, a, b: (a[g], 0, 0)),
                pl.BlockSpec((1, width, features), lambda g, a, b: (b[g], 0, 0)),
                pl.BlockSpec((1, size, 128), lambda g, a, b: (a[g], 0, 0)),
                pl.BlockSpec((1, 8, width), lambda g, a, b: (b[g], 0, 0)),
            ],
            out_specs=pl.BlockSpec((1, size, width), lambda g, a, b: (g, 0, 0)),
        ),
        cost_estimate=pl.CostEstimate(
            flops=2 * n * size * width * features,
            bytes_accessed=2 * n * size * width,
            transcendentals=n * size * width,
        ),
        name="gram",
    )(left_ids, right_ids, left, right, down, across)


def solve_kernel(
    groups, plan, own, offset, piece_rows,
    mine, other, high, low, among, targets, *rest,
):
    tall = rest[:groups]
    residual, steps, losses = rest[groups:groups + 3]
    start, x, wide, cross, high_v, low_v, tall_v, sems, load_sems = rest[groups + 3:]
    rounds, size, width = steps.shape
    rows = residual.shape[0]
    per = rounds // groups
    tiles = rows // size
    count, piece = mine.shape[0], mine.shape[2]

    loads = []

    def load(src, dst):
        copy = pltpu.make_async_copy(src, dst, load_sems.at[len(loads)])
        copy.start()
        loads.append(copy)
        return copy

    ready = []
    pieces = []
    for r in range(rounds):
        mats = [load(high.at[r], high_v.at[r]), load(low.at[r], low_v.at[r])]
        if r > 0:
            first = r * (r - 1) // 2
            mats.append(load(among.at[pl.ds(first, r)], cross.at[pl.ds(first, r)]))
        body = load(tall[r // per].at[pl.ds((r % per) * tiles, tiles)], tall_v.at[r])
        ready.append((mats, body))
    targets_in = load(targets, residual)

    for p in range(count):
        for r in range(rounds):
            start[r, pl.ds(pl.multiple_of(piece_rows[p], piece), piece), :] = mine[p, r]
            start[r, pl.ds(pl.multiple_of(piece_rows[count + p], piece), piece), :] = other[p, r]

    for r in range(rounds):
        mats, body = ready[r]
        for copy in mats:
            copy.wait()
        value = start[r].astype(jnp.float32)
        first = r * (r - 1) // 2
        for s in range(r):
            value = value - jnp.dot(cross[first + s], steps[s], preferred_element_type=jnp.float32)
        x[...] = value
        for s in range(r):
            @pl.when(plan[s] == plan[r])
            def _():
                x[...] = x[...] - RIDGE * wide[s]
        value = x[...]
        top = value.astype(jnp.bfloat16)
        bottom = (value - top.astype(jnp.float32)).astype(jnp.bfloat16)
        step = jnp.dot(high_v[r], top, preferred_element_type=jnp.float32)
        step = step + jnp.dot(low_v[r], top, preferred_element_type=jnp.float32)
        step = step + jnp.dot(high_v[r], bottom, preferred_element_type=jnp.float32)
        wide[r] = step
        steps[r] = step.astype(jnp.bfloat16)

        if r == 0:
            targets_in.wait()
        body.wait()

        @pl.when(own[r] == 1)
        def _():
            where = pl.ds(pl.multiple_of(offset[r], size), size)
            residual[where, :] = residual[where, :] - RIDGE * wide[r]

        total = jnp.zeros((8, width), jnp.float32)
        for t in range(tiles):
            where = pl.ds(t * size, size)
            part = residual[where, :] - jnp.dot(
                tall_v[r, t], steps[r], preferred_element_type=jnp.float32
            )
            residual[where, :] = part
            total = total + jnp.sum((part * part).reshape(size // 8, 8, width), axis=0)
        folded = total[:, 0:128]
        for c in range(1, width // 128):
            folded = folded + total[:, c * 128:(c + 1) * 128]
        losses[r] = folded


def solve(plan, own, offset, piece_rows, mine, other, high, low, among, tall, targets):
    rounds, size, _ = high.shape
    rows, width = targets.shape
    tiles = rows // size
    groups = len(tall)
    n_loads = 4 * rounds
    smem = pl.BlockSpec(memory_space=pltpu.SMEM)
    vmem = pl.BlockSpec(memory_space=pltpu.VMEM)
    far = pl.BlockSpec(memory_space=pl.ANY)
    return pl.pallas_call(
        functools.partial(solve_kernel, groups),
        out_shape=(
            jax.ShapeDtypeStruct((rows, width), jnp.float32),
            jax.ShapeDtypeStruct((rounds, size, width), jnp.bfloat16),
            jax.ShapeDtypeStruct((rounds, 8, 128), jnp.float32),
        ),
        in_specs=[smem] * 4 + [vmem] * 2 + [far] * (4 + groups),
        out_specs=(vmem, vmem, vmem),
        scratch_shapes=[
            pltpu.VMEM((rounds, size, width), jnp.bfloat16),
            pltpu.VMEM((size, width), jnp.float32),
            pltpu.VMEM((rounds, size, width), jnp.float32),
            pltpu.VMEM(among.shape, jnp.bfloat16),
            pltpu.VMEM(high.shape, jnp.bfloat16),
            pltpu.VMEM(low.shape, jnp.bfloat16),
            pltpu.VMEM((rounds, tiles, size, size), jnp.bfloat16),
            pltpu.SemaphoreType.DMA((1,)),
            pltpu.SemaphoreType.DMA((n_loads,)),
        ],
        compiler_params=pltpu.CompilerParams(vmem_limit_bytes=50 * MIB),
        name="solve",
    )(plan, own, offset, piece_rows, mine, other, high, low, among, targets, *tall)


def on_device(mesh_shape, points, targets, plan, block_inverse):
    rows, features = points.shape
    width = targets.shape[1]
    rounds, size, _ = block_inverse.shape
    route = Route(mesh_shape)
    total = rows * route.devices * width
    gamma = 2.0 / features
    norm_scale = -gamma * LOG2E
    inner_scale = 2.0 * gamma * LOG2E
    half = size // 2

    begin = plan * size
    owner = begin // rows
    own = (owner == route.here).astype(jnp.int32)
    offset = jnp.clip(begin - route.here * rows, 0, rows - size)
    staying = offset // half + route.side
    going = offset // half + (1 - route.side)
    piece_rows = route.piece_rows(size)

    points_mine, points_other = route.spread(*pick(points, going, staying, half), owner)
    targets_mine, targets_other = route.spread(*pick(targets, going, staying, half), owner)

    norms, high, low = prepare(points, block_inverse, norm_scale)
    blocks, across, down = assemble(points_mine, points_other, piece_rows, norm_scale)
    tiles = rows // size
    left = points.reshape(tiles, size, features)
    left_norms = norms.reshape(tiles, size, 128)
    tall = []
    per = 2
    for r in range(0, rounds, per):
        pairs = [(t, s) for s in range(r, r + per) for t in range(tiles)]
        tall.append(gram(left, blocks, left_norms, across, pairs, inner_scale))
    among = gram(
        blocks, blocks, down, across, [(r, s) for r in range(rounds) for s in range(r)], inner_scale
    )
    residual, steps, partial = solve(
        plan, own, offset, piece_rows, targets_mine, targets_other, high, low, among, tall, targets
    )
    losses = jnp.sum(route.total(partial), axis=(1, 2)) / total
    return residual, steps, losses


def solution(mesh):
    placed = (P(AXES, None), P(AXES, None), P(), P())
    return jax.shard_map(
        functools.partial(on_device, dict(mesh.shape)),
        mesh=mesh,
        in_specs=placed,
        out_specs=(P(AXES, None), P(), P()),
        check_vma=False,
    )
```

```python
import functools
import math

import jax
import jax.numpy as jnp
from jax import lax
from jax.experimental import pallas as pl
from jax.experimental.pallas import tpu as pltpu
from jax.sharding import PartitionSpec as P

RIDGE = 1.0
AXES = ("row", "col")
HALVINGS = 3
NT = (((1,), (1,)), ((), ()))
LOG2E = math.log2(math.e)
MIB = 1 << 20
SOLVE_VMEM = 16 * MIB
SMEM = pl.BlockSpec(memory_space=pltpu.SMEM)
VMEM = pl.BlockSpec(memory_space=pltpu.VMEM)
HBM = pl.BlockSpec(memory_space=pltpu.HBM)


def stage_bits(mesh_shape, late):
    cols = mesh_shape["col"].bit_length() - 1
    rows = mesh_shape["row"].bit_length() - 1
    core = cols
    along_col = list(range(cols))
    along_row = list(range(cols + 1, cols + rows))
    rest = along_col[2:] + along_row[1:]
    near, far, other = along_col[0], along_col[1], along_row[0]
    if late:
        return core, ([far, near, other] + rest, [far, other, near] + rest)
    return core, ([near, far, other] + rest, [other, near, far] + rest)


def swap(x, devices, bit_of):
    return lax.ppermute(x, AXES, [(i, i ^ (1 << bit_of(i))) for i in range(devices)])


class Route:
    def __init__(self, mesh_shape, late=False):
        self.devices = mesh_shape["row"] * mesh_shape["col"]
        self.core, self.orders = stage_bits(mesh_shape, late)
        self.stages = len(self.orders[0])
        self.halvings = min(HALVINGS, self.stages)
        self.here = lax.axis_index("row") * mesh_shape["col"] + lax.axis_index("col")
        self.side = (self.here >> self.core) & 1

    def swap_core(self, x):
        return swap(x, self.devices, lambda i: self.core)

    def swap_stage(self, x, k):
        return swap(x, self.devices, lambda i: self.orders[(i >> self.core) & 1][k])

    def bit(self, index, k, side=None):
        side = self.side if side is None else side
        first, second = self.orders
        return jnp.where(side == 0, (index >> first[k]) & 1, (index >> second[k]) & 1)

    def piece_rows(self, blocksize):
        count = 1 << self.halvings
        pieces = []
        for side in (self.side, 1 - self.side):
            for p in range(count):
                row = side * (blocksize // 2)
                for k in range(self.halvings):
                    flipped = self.bit(self.here, k, side) ^ ((p >> (self.halvings - 1 - k)) & 1)
                    row = row + flipped * (blocksize >> (k + 2))
                pieces.append(row)
        return pieces

    def spread(self, send, keep, owner):
        recv, = yield (self.swap_core, send),
        mine = keep
        same = ((owner >> self.core) & 1) == self.side
        for k in range(self.halvings):
            bit = self.bit(self.here, k)
            rows = mine.shape[1] // 2

            def half(which):
                return jnp.where(
                    same[:, None, None],
                    lax.dynamic_slice_in_dim(mine, which * rows, rows, 1),
                    lax.dynamic_slice_in_dim(recv, which * rows, rows, 1),
                )

            going, staying = half(1 - bit), half(bit)
            recv, = yield (functools.partial(self.swap_stage, k=k), going),
            mine = staying
            same = self.bit(owner, k) == bit
        for k in range(self.halvings, self.stages):
            mine = jnp.where(same[:, None, None], mine, recv)
            recv, = yield (functools.partial(self.swap_stage, k=k), mine),
            same = self.bit(owner, k) == self.bit(self.here, k)
        mine = jnp.where(same[:, None, None], mine, recv)
        for k in reversed(range(1, self.halvings)):
            recv, = yield (functools.partial(self.swap_stage, k=k), mine),
            mine = jnp.concatenate([mine, recv], 1)
        last = functools.partial(self.swap_stage, k=0)
        recv, mine_over = yield (last, mine), (self.swap_core, mine)
        self.early = mine, mine_over
        recv_over, = yield (self.swap_core, recv),
        return (mine, recv), (mine_over, recv_over)

    def total(self, x):
        x = x + self.swap_core(x)
        for k in range(self.stages):
            x = x + swap(x, self.devices, lambda i: self.orders[0][k])
        return x


class Stream:
    def __init__(self, steps):
        self.steps = steps
        self.result = None
        self.advance(None)

    def advance(self, recv):
        try:
            pairs = self.steps.send(recv)
            self.swaps = [swap for swap, _ in pairs]
            self.sends = tuple(send for _, send in pairs)
        except StopIteration as stop:
            self.swaps = self.sends = ()
            self.result = stop.value

    def go(self):
        self.advance(tuple(swap(send) for swap, send in zip(self.swaps, self.sends)))

    def after(self, *others):
        self.sends, others = lax.optimization_barrier((self.sends, others))
        return others


def together(*streams):
    sends = lax.optimization_barrier(tuple(s.sends for s in streams))
    for stream, ready in zip(streams, sends):
        stream.sends = ready
    for stream in streams:
        stream.go()


def block_offset(plan, r, here, rows, size):
    return pl.multiple_of(jnp.clip(plan[r] * size - here * rows, 0, rows - size), size)


def pick_points_kernel(mesh_shape, plan, points, going, staying, sems):
    slots, half, _ = going.shape
    route = Route(mesh_shape)
    copies = []
    for j, (dst, side) in enumerate(((going, 1 - route.side), (staying, route.side))):
        for r in range(slots):
            at = block_offset(plan, r, route.here, points.shape[0], 2 * half) + side * half
            src = points.at[pl.ds(pl.multiple_of(at, half), half)]
            copies.append(pltpu.make_async_copy(src, dst.at[r], sems.at[j * slots + r]))
            copies[-1].start()
    for copy in copies:
        copy.wait()


def pick_points(mesh_shape, plan, points, size):
    part = pltpu.VMEM((plan.shape[0], size // 2, points.shape[1]), points.dtype)
    return pl.pallas_call(
        functools.partial(pick_points_kernel, mesh_shape),
        out_shape=(part, part),
        in_specs=[SMEM, HBM],
        out_specs=(VMEM, VMEM),
        scratch_shapes=[pltpu.SemaphoreType.DMA((2 * plan.shape[0],))],
        name="pick_points",
    )(plan, points)


def pick_targets_kernel(mesh_shape, plan, targets, going, staying, landing, sems):
    slots, half, _ = going.shape
    route = Route(mesh_shape)
    away = pl.multiple_of((1 - route.side) * half, half)
    stay = pl.multiple_of(route.side * half, half)
    copies = []
    for r in range(slots):
        at = block_offset(plan, r, route.here, targets.shape[0], 2 * half)
        copies.append(pltpu.make_async_copy(
            targets.at[pl.ds(at, 2 * half)], landing.at[r], sems.at[r]))
        copies[-1].start()
    for r in range(slots):
        copies[r].wait()
        going[r] = landing[r, pl.ds(away, half), :].astype(going.dtype)
        staying[r] = landing[r, pl.ds(stay, half), :].astype(staying.dtype)


def pick_targets(mesh_shape, plan, targets, size):
    slots, width = plan.shape[0], targets.shape[1]
    part = pltpu.VMEM((slots, size // 2, width), jnp.bfloat16)
    return pl.pallas_call(
        functools.partial(pick_targets_kernel, mesh_shape),
        out_shape=(part, part),
        in_specs=[SMEM, HBM],
        out_specs=(VMEM, VMEM),
        scratch_shapes=[
            pltpu.VMEM((slots, size, width), targets.dtype),
            pltpu.SemaphoreType.DMA((slots,)),
        ],
        name="pick_targets",
    )(plan, targets)


def lane_sums(p, scale):
    wide = p.astype(jnp.float32)
    sums = scale * jnp.sum(wide * wide, axis=1, keepdims=True)
    return jnp.broadcast_to(sums, (p.shape[0], 128))


def norms_kernel(scale, points, norms):
    norms[...] = lane_sums(points[...], scale)


def point_norms(points, scale):
    rows, features = points.shape
    tile = rows // 2
    return pl.pallas_call(
        functools.partial(norms_kernel, scale),
        out_shape=jax.ShapeDtypeStruct((rows, 128), jnp.float32),
        grid=(rows // tile,),
        in_specs=[pl.BlockSpec((tile, features), lambda t: (t, 0))],
        out_specs=pl.BlockSpec((tile, 128), lambda t: (t, 0)),
        cost_estimate=pl.CostEstimate(flops=0, bytes_accessed=6 * MIB, transcendentals=0),
        name="norms",
    )(points)


def kernel_values(left, right, down, across, scale):
    inner = lax.dot_general(left, right, NT, preferred_element_type=jnp.float32)
    offset = jnp.concatenate([down] * (inner.shape[1] // 128), axis=1) + across
    return jnp.exp2(inner * scale + offset).astype(jnp.bfloat16)


def tall_kernel(norm_scale, scale, mine, other, points, norms, out):
    slots = mine.shape[0]
    tile = points.shape[0] // 2
    for r in range(slots):
        right = jnp.concatenate([mine[r], other[r]], axis=0)
        row = lane_sums(right, norm_scale).T[0:1, :]
        for t in range(2):
            where = pl.ds(t * tile, tile)
            out[r, where, :] = kernel_values(points[where, :], right, norms[where, :], row, scale)


def tall_matrices(points, norms, mine, other, norm_scale, scale):
    slots, quarter, features = mine.shape
    rows = points.shape[0]
    return pl.pallas_call(
        functools.partial(tall_kernel, norm_scale, scale),
        out_shape=pltpu.VMEM((slots, rows, 2 * quarter), jnp.bfloat16),
        in_specs=[VMEM] * 4,
        out_specs=VMEM,
        compiler_params=pltpu.CompilerParams(vmem_limit_bytes=12 * MIB),
        cost_estimate=pl.CostEstimate(
            flops=4 * slots * rows * quarter * features,
            bytes_accessed=8 * slots * rows * quarter,
            transcendentals=2 * slots * rows * quarter,
        ),
        name="tall",
    )(mine, other, points, norms)


def among_kernel(mesh_shape, norm_scale, scale, *refs):
    quarters = refs[0:4]
    out, blocks, down, across = refs[4:]
    rounds, size, _ = blocks.shape
    piece_rows = Route(mesh_shape).piece_rows(size)
    count = len(piece_rows)
    piece = size // count
    per = count // 4
    for r in range(rounds):
        for p in range(count):
            at = pl.multiple_of(piece_rows[p], piece)
            blocks[r, pl.ds(at, piece), :] = quarters[p // per][r, pl.ds(p % per * piece, piece), :]
        sums = lane_sums(blocks[r], norm_scale)
        down[r] = sums
        across[r] = sums.T[0:8, :]
    for s in range(rounds - 1):
        for r in range(s + 1, rounds):
            at = r * (r - 1) // 2 + s
            out[at] = kernel_values(blocks[r], blocks[s], down[r], across[s, 0:1, :], scale)


def among_matrices(mesh_shape, quarters, norm_scale, scale):
    rounds, quarter, features = quarters[0].shape
    size = 4 * quarter
    pairs = rounds * (rounds - 1) // 2
    return pl.pallas_call(
        functools.partial(among_kernel, mesh_shape, norm_scale, scale),
        out_shape=pltpu.VMEM((pairs, size, size), jnp.bfloat16),
        in_specs=[VMEM] * 4,
        out_specs=VMEM,
        scratch_shapes=[
            pltpu.VMEM((rounds, size, features), jnp.bfloat16),
            pltpu.VMEM((rounds, size, 128), jnp.float32),
            pltpu.VMEM((rounds, 8, size), jnp.float32),
        ],
        compiler_params=pltpu.CompilerParams(vmem_limit_bytes=12 * MIB),
        cost_estimate=pl.CostEstimate(
            flops=2 * pairs * size * size * features,
            bytes_accessed=4 * pairs * size * size,
            transcendentals=pairs * size * size,
        ),
        name="among",
    )(*quarters)


def solve_kernel(mesh_shape, plan, *refs):
    quarters = refs[0:4]
    inverse, among, targets, tall_a, tall_b, residual, steps, losses = refs[4:12]
    start, wide, turned = refs[12:]
    rounds, size, width = steps.shape
    rows = residual.shape[0]
    tiles = rows // size
    route = Route(mesh_shape)
    piece_rows = route.piece_rows(size)
    count = len(piece_rows)
    piece = size // count
    per = count // 4

    for r in range(rounds):
        for p in range(count):
            at = pl.multiple_of(piece_rows[p], piece)
            start[r, pl.ds(at, piece), :] = quarters[p // per][r, pl.ds(p % per * piece, piece), :]

    for r in range(rounds):
        value = start[r].astype(jnp.float32)
        first = r * (r - 1) // 2
        for s in range(r):
            value = value - jnp.dot(among[first + s], steps[s], preferred_element_type=jnp.float32)
            value = value - jnp.where(plan[s] == plan[r], RIDGE * wide[s], 0.0)
        top = value.astype(jnp.bfloat16)
        bottom = (value - top.astype(jnp.float32)).astype(jnp.bfloat16)
        matrix = inverse[r]
        high = matrix.astype(jnp.bfloat16)
        low = (matrix - high.astype(jnp.float32)).astype(jnp.bfloat16)
        step = jnp.dot(high, top, preferred_element_type=jnp.float32)
        step = step + jnp.dot(low, top, preferred_element_type=jnp.float32)
        step = step + jnp.dot(high, bottom, preferred_element_type=jnp.float32)
        wide[r] = step
        steps[r] = step.astype(jnp.bfloat16)
        for j, q in enumerate((0, 2, 1, 3)):
            for p in range(per):
                at = pl.multiple_of(piece_rows[q * per + p], piece)
                turned[r, pl.ds((j * per + p) * piece, piece), :] = steps[r, pl.ds(at, piece), :]

        begin = plan[r] * size - route.here * rows
        source = targets if r == 0 else residual
        total = jnp.zeros((8, width), jnp.float32)
        for t in range(tiles):
            where = pl.ds(t * size, size)
            part = source[where, :] - jnp.where(begin == t * size, RIDGE * wide[r], 0.0)
            for j, tall in enumerate((tall_a, tall_b)):
                rhs = turned[r, pl.ds(j * (size // 2), size // 2), :]
                part = part - jnp.dot(tall[r, where, :], rhs, preferred_element_type=jnp.float32)
            residual[where, :] = part
            total = total + jnp.sum((part * part).reshape(size // 8, 8, width), axis=0)
        folded = total[:, 0:128]
        for c in range(1, width // 128):
            folded = folded + total[:, c * 128:(c + 1) * 128]
        losses[r] = folded


def solve(mesh_shape, plan, quarters, inverse, among, tall_a, tall_b, targets):
    rounds, size, _ = inverse.shape
    rows, width = targets.shape
    return pl.pallas_call(
        functools.partial(solve_kernel, mesh_shape),
        out_shape=(
            jax.ShapeDtypeStruct((rows, width), jnp.float32),
            jax.ShapeDtypeStruct((rounds, size, width), jnp.bfloat16),
            jax.ShapeDtypeStruct((rounds, 8, 128), jnp.float32),
        ),
        in_specs=[SMEM] + [VMEM] * 9,
        out_specs=(VMEM, VMEM, VMEM),
        scratch_shapes=[
            pltpu.VMEM((rounds, size, width), jnp.bfloat16),
            pltpu.VMEM((rounds, size, width), jnp.float32),
            pltpu.VMEM((rounds, size, width), jnp.bfloat16),
        ],
        compiler_params=pltpu.CompilerParams(vmem_limit_bytes=SOLVE_VMEM),
        name="solve",
    )(plan, *quarters, inverse, among, targets, tall_a, tall_b)


def on_device(mesh_shape, points, targets, plan, block_inverse):
    rows, features = points.shape
    width = targets.shape[1]
    size = block_inverse.shape[1]
    route = Route(mesh_shape)
    total = rows * route.devices * width
    gamma = 2.0 / features
    norm_scale = -gamma * LOG2E
    inner_scale = 2.0 * gamma * LOG2E

    owner = plan * size // rows

    lead = Stream(route.spread(*pick_points(mesh_shape, plan, points, size), owner))
    trail = None
    tall_a = None
    stage = 0
    while lead.result is None:
        if stage == 1:
            held, = lead.after(targets)
            trail = Stream(route.spread(*pick_targets(mesh_shape, plan, held, size), owner))
        if stage == 2:
            held, = lead.after(points)
            norms = point_norms(held, norm_scale)
        if stage == 3:
            norms, = lead.after(norms)
        if hasattr(route, "early") and tall_a is None:
            tall_a = tall_matrices(points, norms, *route.early, norm_scale, inner_scale)
            tall_a, = lead.after(tall_a)
        if stage == 0:
            lead.go()
        elif stage == 1:
            lead.go()
            trail.go()
        else:
            together(lead, trail)
        stage += 1
    (first_mine, last_mine), (first_other, last_other) = lead.result

    if trail.result is None:
        last_mine, = trail.after(last_mine)
    tall_b = tall_matrices(points, norms, last_mine, last_other, norm_scale, inner_scale)
    ready = (first_mine, last_mine, first_other, last_other)
    if trail.result is None:
        trail.go()
        if trail.result is None:
            tall_b, ready = trail.after(tall_b, ready)
    among = among_matrices(mesh_shape, ready, norm_scale, inner_scale)
    while trail.result is None:
        trail.go()
    (a, b), (c, d) = trail.result
    residual, steps, partial = solve(
        mesh_shape, plan, (a, b, c, d), block_inverse, among, tall_a, tall_b, targets)
    losses = jnp.sum(route.total(partial), axis=(1, 2)) / total
    return residual, steps, losses


def solution(mesh):
    placed = (P(AXES, None), P(AXES, None), P(), P())
    return jax.shard_map(
        functools.partial(on_device, dict(mesh.shape)),
        mesh=mesh,
        in_specs=placed,
        out_specs=(P(AXES, None), P(), P()),
        check_vma=False,
    )
```

```python
import functools
import math

import jax
import jax.numpy as jnp
from jax import lax
from jax.experimental import pallas as pl
from jax.experimental.pallas import tpu as pltpu
from jax.sharding import PartitionSpec as P

RIDGE = 1.0
AXES = ("row", "col")
HALVINGS = 3
NT = (((1,), (1,)), ((), ()))
LOG2E = math.log2(math.e)
MIB = 1 << 20
SOLVE_VMEM = 16 * MIB
SMEM = pl.BlockSpec(memory_space=pltpu.SMEM)
VMEM = pl.BlockSpec(memory_space=pltpu.VMEM)
HBM = pl.BlockSpec(memory_space=pltpu.HBM)


def stage_bits(mesh_shape, late):
    cols = mesh_shape["col"].bit_length() - 1
    rows = mesh_shape["row"].bit_length() - 1
    core = cols
    along_col = list(range(cols))
    along_row = list(range(cols + 1, cols + rows))
    rest = along_col[2:] + along_row[1:]
    near, far, other = along_col[0], along_col[1], along_row[0]
    if late:
        return core, ([far, near, other] + rest, [far, other, near] + rest)
    return core, ([near, far, other] + rest, [other, near, far] + rest)


def swap(x, devices, bit_of):
    return lax.ppermute(x, AXES, [(i, i ^ (1 << bit_of(i))) for i in range(devices)])


class Route:
    def __init__(self, mesh_shape, late=False):
        self.mesh_shape = mesh_shape
        self.blocks = mesh_shape.get("blocks", 1)
        self.devices = mesh_shape["row"] * mesh_shape["col"]
        self.core, self.orders = stage_bits(mesh_shape, late)
        self.stages = len(self.orders[0])
        self.halvings = min(HALVINGS, self.stages)
        self.here = lax.axis_index("row") * mesh_shape["col"] + lax.axis_index("col")
        self.side = (self.here >> self.core) & 1

    def owner(self, block):
        return lax.div(block, self.blocks)

    def swap_core(self, x):
        return swap(x, self.devices, lambda i: self.core)

    def swap_stage(self, x, k):
        return swap(x, self.devices, lambda i: self.orders[(i >> self.core) & 1][k])

    def bit(self, index, k, side=None):
        side = self.side if side is None else side
        first, second = self.orders
        return jnp.where(side == 0, (index >> first[k]) & 1, (index >> second[k]) & 1)

    def piece_rows(self, blocksize):
        count = 1 << self.halvings
        pieces = []
        for side in (self.side, 1 - self.side):
            for p in range(count):
                row = side * (blocksize // 2)
                for k in range(self.halvings):
                    flipped = self.bit(self.here, k, side) ^ ((p >> (self.halvings - 1 - k)) & 1)
                    row = row + flipped * (blocksize >> (k + 2))
                pieces.append(row)
        return pieces

    def spread(self, send, keep, plan, owner):
        recv, = yield (self.swap_core, send),
        mine = keep
        same = ((owner >> self.core) & 1) == self.side
        for k in range(self.halvings):
            bit = self.bit(self.here, k)
            rows = mine.shape[1] // 2

            def half(which):
                return jnp.where(
                    same[:, None, None],
                    lax.dynamic_slice_in_dim(mine, which * rows, rows, 1),
                    lax.dynamic_slice_in_dim(recv, which * rows, rows, 1),
                )

            if k < 2 and mine.shape[2] > 256:
                going, staying = halve(self.mesh_shape, k, plan, mine, recv)
            else:
                going, staying = half(1 - bit), half(bit)
            recv, = yield (functools.partial(self.swap_stage, k=k), going),
            mine = staying
            same = self.bit(owner, k) == bit
        for k in range(self.halvings, self.stages):
            mine = jnp.where(same[:, None, None], mine, recv)
            recv, = yield (functools.partial(self.swap_stage, k=k), mine),
            same = self.bit(owner, k) == self.bit(self.here, k)
        mine = jnp.where(same[:, None, None], mine, recv)
        for k in reversed(range(1, self.halvings)):
            recv, = yield (functools.partial(self.swap_stage, k=k), mine),
            mine = jnp.concatenate([mine, recv], 1)
        last = functools.partial(self.swap_stage, k=0)
        recv, mine_over = yield (last, mine), (self.swap_core, mine)
        self.early = mine, mine_over
        recv_over, = yield (self.swap_core, recv),
        return (mine, recv), (mine_over, recv_over)

    def total(self, x):
        x = x + self.swap_core(x)
        for k in range(self.stages):
            x = x + swap(x, self.devices, lambda i: self.orders[0][k])
        return x


class Stream:
    def __init__(self, steps):
        self.steps = steps
        self.result = None
        self.advance(None)

    def advance(self, recv):
        try:
            pairs = self.steps.send(recv)
            self.swaps = [swap for swap, _ in pairs]
            self.sends = tuple(send for _, send in pairs)
        except StopIteration as stop:
            self.swaps = self.sends = ()
            self.result = stop.value

    def go(self):
        self.advance(tuple(swap(send) for swap, send in zip(self.swaps, self.sends)))

    def after(self, *others):
        self.sends, others = lax.optimization_barrier((self.sends, others))
        return others


def together(lead, trail, before):
    if before is not None:
        lead.sends, _ = lax.optimization_barrier((lead.sends, before))
    trail.sends, _ = lax.optimization_barrier((trail.sends, lead.sends))
    before = trail.sends
    lead.go()
    trail.go()
    return before


def block_offset(plan, r, here, rows, size):
    return pl.multiple_of(jnp.clip(plan[r] * size - here * rows, 0, rows - size), size)


def pick_points_kernel(mesh_shape, plan, points, going, staying, sems):
    slots, half, _ = going.shape
    route = Route(mesh_shape)
    copies = []
    for j, (dst, side) in enumerate(((going, 1 - route.side), (staying, route.side))):
        for r in range(slots):
            at = block_offset(plan, r, route.here, points.shape[0], 2 * half) + side * half
            src = points.at[pl.ds(pl.multiple_of(at, half), half)]
            copies.append(pltpu.make_async_copy(src, dst.at[r], sems.at[j * slots + r]))
            copies[-1].start()
    for copy in copies:
        copy.wait()


def pick_points(mesh_shape, plan, points, size):
    part = pltpu.VMEM((plan.shape[0], size // 2, points.shape[1]), points.dtype)
    return pl.pallas_call(
        functools.partial(pick_points_kernel, mesh_shape),
        out_shape=(part, part),
        in_specs=[SMEM, HBM],
        out_specs=(VMEM, VMEM),
        scratch_shapes=[pltpu.SemaphoreType.DMA((2 * plan.shape[0],))],
        name="pick_points",
    )(plan, points)


def halve_kernel(mesh_shape, k, plan, mine, recv, going, staying):
    slots, rows, _ = going.shape
    route = Route(mesh_shape)
    bit = route.bit(route.here, k)
    for r in range(slots):
        owner = route.owner(plan[r])
        if k == 0:
            same = ((owner >> route.core) & 1) == route.side
        else:
            same = route.bit(owner, k - 1) == route.bit(route.here, k - 1)
        for dst, which in ((going, 1 - bit), (staying, bit)):
            part = pl.ds(pl.multiple_of(which * rows, rows), rows)

            @pl.when(same)
            def _():
                dst[r] = mine[r, part, :]

            @pl.when(jnp.logical_not(same))
            def _():
                dst[r] = recv[r, part, :]


def halve(mesh_shape, k, plan, mine, recv):
    slots, rows, width = recv.shape
    part = jax.ShapeDtypeStruct((slots, rows // 2, width), recv.dtype)
    return pl.pallas_call(
        functools.partial(halve_kernel, mesh_shape, k),
        out_shape=(part, part),
        in_specs=[SMEM, VMEM, VMEM],
        out_specs=(VMEM, VMEM),
        compiler_params=pltpu.CompilerParams(vmem_limit_bytes=8 * MIB),
        name="halve",
    )(plan, mine, recv)


def pick_targets_kernel(mesh_shape, plan, targets, going, staying, landing, sems):
    slots, half, _ = going.shape
    route = Route(mesh_shape)
    away = pl.multiple_of((1 - route.side) * half, half)
    stay = pl.multiple_of(route.side * half, half)
    copies = []
    for r in range(slots):
        at = block_offset(plan, r, route.here, targets.shape[0], 2 * half)
        copies.append(pltpu.make_async_copy(
            targets.at[pl.ds(at, 2 * half)], landing.at[r], sems.at[r]))
        copies[-1].start()
    for r in range(slots):
        copies[r].wait()
        going[r] = landing[r, pl.ds(away, half), :].astype(going.dtype)
        staying[r] = landing[r, pl.ds(stay, half), :].astype(staying.dtype)


def pick_targets(mesh_shape, plan, targets, size):
    slots, width = plan.shape[0], targets.shape[1]
    part = pltpu.VMEM((slots, size // 2, width), jnp.bfloat16)
    return pl.pallas_call(
        functools.partial(pick_targets_kernel, mesh_shape),
        out_shape=(part, part),
        in_specs=[SMEM, HBM],
        out_specs=(VMEM, VMEM),
        scratch_shapes=[
            pltpu.VMEM((slots, size, width), targets.dtype),
            pltpu.SemaphoreType.DMA((slots,)),
        ],
        name="pick_targets",
    )(plan, targets)


def lane_sums(p, scale):
    wide = p.astype(jnp.float32)
    sums = scale * jnp.sum(wide * wide, axis=1, keepdims=True)
    return jnp.broadcast_to(sums, (p.shape[0], 128))


def norms_kernel(scale, points, norms):
    norms[...] = lane_sums(points[...], scale)


def point_norms(points, scale):
    rows, features = points.shape
    tile = rows // 2
    return pl.pallas_call(
        functools.partial(norms_kernel, scale),
        out_shape=jax.ShapeDtypeStruct((rows, 128), jnp.float32),
        grid=(rows // tile,),
        in_specs=[pl.BlockSpec((tile, features), lambda t: (t, 0))],
        out_specs=pl.BlockSpec((tile, 128), lambda t: (t, 0)),
        cost_estimate=pl.CostEstimate(flops=0, bytes_accessed=6 * MIB, transcendentals=0),
        name="norms",
    )(points)


def kernel_values(left, right, down, across, scale):
    inner = lax.dot_general(left, right, NT, preferred_element_type=jnp.float32)
    offset = jnp.concatenate([down] * (inner.shape[1] // 128), axis=1) + across
    return jnp.exp2(inner * scale + offset).astype(jnp.bfloat16)


def tall_kernel(norm_scale, scale, mine, other, points, norms, out):
    slots = mine.shape[0]
    tile = points.shape[0] // 2
    for r in range(slots):
        right = jnp.concatenate([mine[r], other[r]], axis=0)
        row = lane_sums(right, norm_scale).T[0:1, :]
        for t in range(2):
            where = pl.ds(t * tile, tile)
            out[r, where, :] = kernel_values(points[where, :], right, norms[where, :], row, scale)


def tall_matrices(points, norms, mine, other, norm_scale, scale):
    slots, quarter, features = mine.shape
    rows = points.shape[0]
    return pl.pallas_call(
        functools.partial(tall_kernel, norm_scale, scale),
        out_shape=pltpu.VMEM((slots, rows, 2 * quarter), jnp.bfloat16),
        in_specs=[VMEM] * 4,
        out_specs=VMEM,
        compiler_params=pltpu.CompilerParams(vmem_limit_bytes=12 * MIB),
        cost_estimate=pl.CostEstimate(
            flops=4 * slots * rows * quarter * features,
            bytes_accessed=8 * slots * rows * quarter,
            transcendentals=2 * slots * rows * quarter,
        ),
        name="tall",
    )(mine, other, points, norms)


def among_kernel(mesh_shape, norm_scale, scale, *refs):
    quarters = refs[0:4]
    out, blocks, down, across = refs[4:]
    rounds, size, _ = blocks.shape
    piece_rows = Route(mesh_shape).piece_rows(size)
    count = len(piece_rows)
    piece = size // count
    per = count // 4
    for r in range(rounds):
        for p in range(count):
            at = pl.multiple_of(piece_rows[p], piece)
            blocks[r, pl.ds(at, piece), :] = quarters[p // per][r, pl.ds(p % per * piece, piece), :]
        sums = lane_sums(blocks[r], norm_scale)
        down[r] = sums
        across[r] = sums.T[0:8, :]
    for s in range(rounds - 1):
        for r in range(s + 1, rounds):
            at = r * (r - 1) // 2 + s
            out[at] = kernel_values(blocks[r], blocks[s], down[r], across[s, 0:1, :], scale)


def among_matrices(mesh_shape, quarters, norm_scale, scale):
    rounds, quarter, features = quarters[0].shape
    size = 4 * quarter
    pairs = rounds * (rounds - 1) // 2
    return pl.pallas_call(
        functools.partial(among_kernel, mesh_shape, norm_scale, scale),
        out_shape=pltpu.VMEM((pairs, size, size), jnp.bfloat16),
        in_specs=[VMEM] * 4,
        out_specs=VMEM,
        scratch_shapes=[
            pltpu.VMEM((rounds, size, features), jnp.bfloat16),
            pltpu.VMEM((rounds, size, 128), jnp.float32),
            pltpu.VMEM((rounds, 8, size), jnp.float32),
        ],
        compiler_params=pltpu.CompilerParams(vmem_limit_bytes=12 * MIB),
        cost_estimate=pl.CostEstimate(
            flops=2 * pairs * size * size * features,
            bytes_accessed=4 * pairs * size * size,
            transcendentals=pairs * size * size,
        ),
        name="among",
    )(*quarters)


def solve_kernel(mesh_shape, plan, *refs):
    quarters = refs[0:4]
    inverse, among, targets, tall_a, tall_b, residual, steps, losses = refs[4:12]
    start, wide, turned = refs[12:]
    rounds, size, width = steps.shape
    rows = residual.shape[0]
    tiles = rows // size
    route = Route(mesh_shape)
    piece_rows = route.piece_rows(size)
    count = len(piece_rows)
    piece = size // count
    per = count // 4

    for r in range(rounds):
        for p in range(count):
            at = pl.multiple_of(piece_rows[p], piece)
            start[r, pl.ds(at, piece), :] = quarters[p // per][r, pl.ds(p % per * piece, piece), :]

    for r in range(rounds):
        value = start[r].astype(jnp.float32)
        first = r * (r - 1) // 2
        for s in range(r):
            value = value - jnp.dot(among[first + s], steps[s], preferred_element_type=jnp.float32)
            value = value - jnp.where(plan[s] == plan[r], RIDGE * wide[s], 0.0)
        top = value.astype(jnp.bfloat16)
        matrix = inverse[r]
        high = matrix.astype(jnp.bfloat16)
        low = (matrix - high.astype(jnp.float32)).astype(jnp.bfloat16)
        step = jnp.dot(high, top, preferred_element_type=jnp.float32)
        step = step + jnp.dot(low, top, preferred_element_type=jnp.float32)
        wide[r] = step
        steps[r] = step.astype(jnp.bfloat16)
        for j, q in enumerate((0, 2, 1, 3)):
            for p in range(per):
                at = pl.multiple_of(piece_rows[q * per + p], piece)
                turned[r, pl.ds((j * per + p) * piece, piece), :] = steps[r, pl.ds(at, piece), :]

        begin = plan[r] * size - route.here * rows
        source = targets if r == 0 else residual
        total = jnp.zeros((8, width), jnp.float32)
        for t in range(tiles):
            where = pl.ds(t * size, size)
            part = source[where, :] - jnp.where(begin == t * size, RIDGE * wide[r], 0.0)
            for j, tall in enumerate((tall_a, tall_b)):
                rhs = turned[r, pl.ds(j * (size // 2), size // 2), :]
                part = part - jnp.dot(tall[r, where, :], rhs, preferred_element_type=jnp.float32)
            residual[where, :] = part
            total = total + jnp.sum((part * part).reshape(size // 8, 8, width), axis=0)
        folded = total[:, 0:128]
        for c in range(1, width // 128):
            folded = folded + total[:, c * 128:(c + 1) * 128]
        losses[r] = folded


def solve(mesh_shape, plan, quarters, inverse, among, tall_a, tall_b, targets):
    rounds, size, _ = inverse.shape
    rows, width = targets.shape
    return pl.pallas_call(
        functools.partial(solve_kernel, mesh_shape),
        out_shape=(
            jax.ShapeDtypeStruct((rows, width), jnp.float32),
            jax.ShapeDtypeStruct((rounds, size, width), jnp.bfloat16),
            jax.ShapeDtypeStruct((rounds, 8, 128), jnp.float32),
        ),
        in_specs=[SMEM] + [VMEM] * 9,
        out_specs=(VMEM, VMEM, VMEM),
        scratch_shapes=[
            pltpu.VMEM((rounds, size, width), jnp.bfloat16),
            pltpu.VMEM((rounds, size, width), jnp.float32),
            pltpu.VMEM((rounds, size, width), jnp.bfloat16),
        ],
        compiler_params=pltpu.CompilerParams(vmem_limit_bytes=SOLVE_VMEM),
        name="solve",
    )(plan, *quarters, inverse, among, targets, tall_a, tall_b)


def on_device(mesh_shape, points, targets, plan, block_inverse):
    rows, features = points.shape
    width = targets.shape[1]
    size = block_inverse.shape[1]
    mesh_shape = dict(mesh_shape, blocks=rows // size)
    route = Route(mesh_shape)
    total = rows * route.devices * width
    gamma = 2.0 / features
    norm_scale = -gamma * LOG2E
    inner_scale = 2.0 * gamma * LOG2E

    owner = plan * size // rows

    lead = Stream(route.spread(*pick_points(mesh_shape, plan, points, size), plan, owner))
    trail = None
    before = None
    tall_a = None
    stage = 0
    while lead.result is None:
        if stage == 1:
            held, = lead.after(targets)
            trail = Stream(route.spread(*pick_targets(mesh_shape, plan, held, size), plan, owner))
        if stage == 2:
            held, = lead.after(points)
            norms = point_norms(held, norm_scale)
        if stage == 3:
            norms, = lead.after(norms)
        if hasattr(route, "early") and tall_a is None:
            tall_a = tall_matrices(points, norms, *route.early, norm_scale, inner_scale)
            tall_a, = lead.after(tall_a)
        if stage == 0:
            lead.go()
        elif stage == 1:
            lead.go()
            trail.go()
        else:
            before = together(lead, trail, before)
        stage += 1
    (first_mine, last_mine), (first_other, last_other) = lead.result

    tall_b = tall_matrices(points, norms, last_mine, last_other, norm_scale, inner_scale)
    if trail.result is None:
        tall_b, = trail.after(tall_b)
        trail.go()
    ready = (first_mine, last_mine, first_other, last_other)
    among = among_matrices(mesh_shape, ready, norm_scale, inner_scale)
    while trail.result is None:
        trail.go()
    (a, b), (c, d) = trail.result
    residual, steps, partial = solve(
        mesh_shape, plan, (a, b, c, d), block_inverse, among, tall_a, tall_b, targets)
    losses = jnp.sum(route.total(partial), axis=(1, 2)) / total
    return residual, steps, losses


def solution(mesh):
    placed = (P(AXES, None), P(AXES, None), P(), P())
    return jax.shard_map(
        functools.partial(on_device, dict(mesh.shape)),
        mesh=mesh,
        in_specs=placed,
        out_specs=(P(AXES, None), P(), P()),
        check_vma=False,
    )
```

```python
import functools
import math

import jax
import jax.numpy as jnp
from jax import lax
from jax.experimental import pallas as pl
from jax.experimental.pallas import tpu as pltpu
from jax.sharding import PartitionSpec as P

RIDGE = 1.0
AXES = ("row", "col")
HALVINGS = 3
NT = (((1,), (1,)), ((), ()))
LOG2E = math.log2(math.e)
MIB = 1 << 20
SOLVE_VMEM = 16 * MIB
SMEM = pl.BlockSpec(memory_space=pltpu.SMEM)
VMEM = pl.BlockSpec(memory_space=pltpu.VMEM)
HBM = pl.BlockSpec(memory_space=pltpu.HBM)


def stage_bits(mesh_shape, late):
    cols = mesh_shape["col"].bit_length() - 1
    rows = mesh_shape["row"].bit_length() - 1
    core = cols
    along_col = list(range(cols))
    along_row = list(range(cols + 1, cols + rows))
    rest = along_col[2:] + along_row[1:]
    near, far, other = along_col[0], along_col[1], along_row[0]
    if late:
        return core, ([far, near, other] + rest, [far, other, near] + rest)
    return core, ([near, far, other] + rest, [other, near, far] + rest)


def swap(x, devices, bit_of):
    return lax.ppermute(x, AXES, [(i, i ^ (1 << bit_of(i))) for i in range(devices)])


class Route:
    def __init__(self, mesh_shape, late=False):
        self.mesh_shape = mesh_shape
        self.blocks = mesh_shape.get("blocks", 1)
        self.devices = mesh_shape["row"] * mesh_shape["col"]
        self.core, self.orders = stage_bits(mesh_shape, late)
        self.stages = len(self.orders[0])
        self.halvings = min(HALVINGS, self.stages)
        self.here = lax.axis_index("row") * mesh_shape["col"] + lax.axis_index("col")
        self.side = (self.here >> self.core) & 1

    def owner(self, block):
        return lax.div(block, self.blocks)

    def swap_core(self, x):
        return swap(x, self.devices, lambda i: self.core)

    def swap_stage(self, x, k):
        return swap(x, self.devices, lambda i: self.orders[(i >> self.core) & 1][k])

    def bit(self, index, k, side=None):
        side = self.side if side is None else side
        first, second = self.orders
        return jnp.where(side == 0, (index >> first[k]) & 1, (index >> second[k]) & 1)

    def piece_rows(self, blocksize):
        count = 1 << self.halvings
        pieces = []
        for side in (self.side, 1 - self.side):
            for p in range(count):
                row = side * (blocksize // 2)
                for k in range(self.halvings):
                    flipped = self.bit(self.here, k, side) ^ ((p >> (self.halvings - 1 - k)) & 1)
                    row = row + flipped * (blocksize >> (k + 2))
                pieces.append(row)
        return pieces

    def spread(self, send, keep, plan, owner):
        recv, = yield (self.swap_core, send),
        mine = keep
        same = ((owner >> self.core) & 1) == self.side
        for k in range(self.halvings):
            bit = self.bit(self.here, k)
            rows = mine.shape[1] // 2

            def half(which):
                return jnp.where(
                    same[:, None, None],
                    lax.dynamic_slice_in_dim(mine, which * rows, rows, 1),
                    lax.dynamic_slice_in_dim(recv, which * rows, rows, 1),
                )

            if k < 2 and mine.shape[2] > 256:
                going, staying = halve(self.mesh_shape, k, plan, mine, recv)
            else:
                going, staying = half(1 - bit), half(bit)
            recv, = yield (functools.partial(self.swap_stage, k=k), going),
            mine = staying
            same = self.bit(owner, k) == bit
        for k in range(self.halvings, self.stages):
            mine = jnp.where(same[:, None, None], mine, recv)
            recv, = yield (functools.partial(self.swap_stage, k=k), mine),
            same = self.bit(owner, k) == self.bit(self.here, k)
        mine = jnp.where(same[:, None, None], mine, recv)
        for k in reversed(range(1, self.halvings)):
            recv, = yield (functools.partial(self.swap_stage, k=k), mine),
            mine = jnp.concatenate([mine, recv], 1)
        last = functools.partial(self.swap_stage, k=0)
        recv, mine_over = yield (last, mine), (self.swap_core, mine)
        self.early = mine, mine_over
        recv_over, = yield (self.swap_core, recv),
        return (mine, recv), (mine_over, recv_over)

    def total(self, x):
        x = x + self.swap_core(x)
        for k in range(self.stages):
            x = x + swap(x, self.devices, lambda i: self.orders[0][k])
        return x


class Stream:
    def __init__(self, steps):
        self.steps = steps
        self.result = None
        self.advance(None)

    def advance(self, recv):
        try:
            pairs = self.steps.send(recv)
            self.swaps = [swap for swap, _ in pairs]
            self.sends = tuple(send for _, send in pairs)
        except StopIteration as stop:
            self.swaps = self.sends = ()
            self.result = stop.value

    def go(self):
        self.advance(tuple(swap(send) for swap, send in zip(self.swaps, self.sends)))

    def after(self, *others):
        self.sends, others = lax.optimization_barrier((self.sends, others))
        return others


def together(lead, trail, before):
    if before is not None:
        lead.sends, _ = lax.optimization_barrier((lead.sends, before))
    trail.sends, _ = lax.optimization_barrier((trail.sends, lead.sends))
    before = trail.sends
    lead.go()
    trail.go()
    return before


def block_offset(plan, r, here, rows, size):
    return pl.multiple_of(jnp.clip(plan[r] * size - here * rows, 0, rows - size), size)


def pick_points_kernel(mesh_shape, plan, points, going, staying, sems):
    slots, half, _ = going.shape
    route = Route(mesh_shape)
    copies = []
    for j, (dst, side) in enumerate(((going, 1 - route.side), (staying, route.side))):
        for r in range(slots):
            at = block_offset(plan, r, route.here, points.shape[0], 2 * half) + side * half
            src = points.at[pl.ds(pl.multiple_of(at, half), half)]
            copies.append(pltpu.make_async_copy(src, dst.at[r], sems.at[j * slots + r]))
            copies[-1].start()
    for copy in copies:
        copy.wait()


def pick_points(mesh_shape, plan, points, size):
    part = pltpu.VMEM((plan.shape[0], size // 2, points.shape[1]), points.dtype)
    return pl.pallas_call(
        functools.partial(pick_points_kernel, mesh_shape),
        out_shape=(part, part),
        in_specs=[SMEM, HBM],
        out_specs=(VMEM, VMEM),
        scratch_shapes=[pltpu.SemaphoreType.DMA((2 * plan.shape[0],))],
        name="pick_points",
    )(plan, points)


def halve_kernel(mesh_shape, k, plan, mine, recv, going, staying):
    slots, rows, _ = going.shape
    route = Route(mesh_shape)
    bit = route.bit(route.here, k)
    for r in range(slots):
        owner = route.owner(plan[r])
        if k == 0:
            same = ((owner >> route.core) & 1) == route.side
        else:
            same = route.bit(owner, k - 1) == route.bit(route.here, k - 1)
        for dst, which in ((going, 1 - bit), (staying, bit)):
            part = pl.ds(pl.multiple_of(which * rows, rows), rows)

            @pl.when(same)
            def _():
                dst[r] = mine[r, part, :]

            @pl.when(jnp.logical_not(same))
            def _():
                dst[r] = recv[r, part, :]


def halve(mesh_shape, k, plan, mine, recv):
    slots, rows, width = recv.shape
    part = jax.ShapeDtypeStruct((slots, rows // 2, width), recv.dtype)
    return pl.pallas_call(
        functools.partial(halve_kernel, mesh_shape, k),
        out_shape=(part, part),
        in_specs=[SMEM, VMEM, VMEM],
        out_specs=(VMEM, VMEM),
        compiler_params=pltpu.CompilerParams(vmem_limit_bytes=8 * MIB),
        name="halve",
    )(plan, mine, recv)


def pick_targets_kernel(mesh_shape, plan, targets, going, staying, landing, sems):
    slots, half, _ = going.shape
    route = Route(mesh_shape)
    away = pl.multiple_of((1 - route.side) * half, half)
    stay = pl.multiple_of(route.side * half, half)
    copies = []
    for r in range(slots):
        at = block_offset(plan, r, route.here, targets.shape[0], 2 * half)
        copies.append(pltpu.make_async_copy(
            targets.at[pl.ds(at, 2 * half)], landing.at[r], sems.at[r]))
        copies[-1].start()
    for r in range(slots):
        copies[r].wait()
        going[r] = landing[r, pl.ds(away, half), :].astype(going.dtype)
        staying[r] = landing[r, pl.ds(stay, half), :].astype(staying.dtype)


def pick_targets(mesh_shape, plan, targets, size):
    slots, width = plan.shape[0], targets.shape[1]
    part = pltpu.VMEM((slots, size // 2, width), jnp.bfloat16)
    return pl.pallas_call(
        functools.partial(pick_targets_kernel, mesh_shape),
        out_shape=(part, part),
        in_specs=[SMEM, HBM],
        out_specs=(VMEM, VMEM),
        scratch_shapes=[
            pltpu.VMEM((slots, size, width), targets.dtype),
            pltpu.SemaphoreType.DMA((slots,)),
        ],
        name="pick_targets",
    )(plan, targets)


def lane_sums(p, scale):
    wide = p.astype(jnp.float32)
    sums = scale * jnp.sum(wide * wide, axis=1, keepdims=True)
    return jnp.broadcast_to(sums, (p.shape[0], 128))


def norms_kernel(scale, points, norms):
    norms[...] = lane_sums(points[...], scale)


def point_norms(points, scale):
    rows, features = points.shape
    tile = rows // 2
    return pl.pallas_call(
        functools.partial(norms_kernel, scale),
        out_shape=jax.ShapeDtypeStruct((rows, 128), jnp.float32),
        grid=(rows // tile,),
        in_specs=[pl.BlockSpec((tile, features), lambda t: (t, 0))],
        out_specs=pl.BlockSpec((tile, 128), lambda t: (t, 0)),
        cost_estimate=pl.CostEstimate(flops=0, bytes_accessed=6 * MIB, transcendentals=0),
        name="norms",
    )(points)


def kernel_values(left, right, down, across, scale):
    inner = lax.dot_general(left, right, NT, preferred_element_type=jnp.float32)
    offset = jnp.concatenate([down] * (inner.shape[1] // 128), axis=1) + across
    return jnp.exp2(inner * scale + offset).astype(jnp.bfloat16)


def tall_kernel(norm_scale, scale, mine, other, points, norms, out):
    slots = mine.shape[0]
    tile = points.shape[0] // 2
    for r in range(slots):
        right = jnp.concatenate([mine[r], other[r]], axis=0)
        row = lane_sums(right, norm_scale).T[0:1, :]
        for t in range(2):
            where = pl.ds(t * tile, tile)
            out[r, where, :] = kernel_values(points[where, :], right, norms[where, :], row, scale)


def tall_matrices(points, norms, mine, other, norm_scale, scale):
    slots, quarter, features = mine.shape
    rows = points.shape[0]
    return pl.pallas_call(
        functools.partial(tall_kernel, norm_scale, scale),
        out_shape=pltpu.VMEM((slots, rows, 2 * quarter), jnp.bfloat16),
        in_specs=[VMEM] * 4,
        out_specs=VMEM,
        compiler_params=pltpu.CompilerParams(vmem_limit_bytes=12 * MIB),
        cost_estimate=pl.CostEstimate(
            flops=4 * slots * rows * quarter * features,
            bytes_accessed=8 * slots * rows * quarter,
            transcendentals=2 * slots * rows * quarter,
        ),
        name="tall",
    )(mine, other, points, norms)


def among_kernel(mesh_shape, norm_scale, scale, *refs):
    quarters = refs[0:4]
    out, blocks, down, across = refs[4:]
    rounds, size, _ = blocks.shape
    piece_rows = Route(mesh_shape).piece_rows(size)
    count = len(piece_rows)
    piece = size // count
    per = count // 4
    for r in range(rounds):
        for p in range(count):
            at = pl.multiple_of(piece_rows[p], piece)
            blocks[r, pl.ds(at, piece), :] = quarters[p // per][r, pl.ds(p % per * piece, piece), :]
        sums = lane_sums(blocks[r], norm_scale)
        down[r] = sums
        across[r] = sums.T[0:8, :]
    for s in range(rounds - 1):
        for r in range(s + 1, rounds):
            at = r * (r - 1) // 2 + s
            out[at] = kernel_values(blocks[r], blocks[s], down[r], across[s, 0:1, :], scale)


def among_matrices(mesh_shape, quarters, norm_scale, scale):
    rounds, quarter, features = quarters[0].shape
    size = 4 * quarter
    pairs = rounds * (rounds - 1) // 2
    return pl.pallas_call(
        functools.partial(among_kernel, mesh_shape, norm_scale, scale),
        out_shape=pltpu.VMEM((pairs, size, size), jnp.bfloat16),
        in_specs=[VMEM] * 4,
        out_specs=VMEM,
        scratch_shapes=[
            pltpu.VMEM((rounds, size, features), jnp.bfloat16),
            pltpu.VMEM((rounds, size, 128), jnp.float32),
            pltpu.VMEM((rounds, 8, size), jnp.float32),
        ],
        compiler_params=pltpu.CompilerParams(vmem_limit_bytes=12 * MIB),
        cost_estimate=pl.CostEstimate(
            flops=2 * pairs * size * size * features,
            bytes_accessed=4 * pairs * size * size,
            transcendentals=pairs * size * size,
        ),
        name="among",
    )(*quarters)


def solve_kernel(mesh_shape, plan, *refs):
    quarters = refs[0:4]
    inverse, among, targets, tall_a, tall_b, residual, steps, losses = refs[4:12]
    start, wide, turned = refs[12:]
    rounds, size, width = steps.shape
    rows = residual.shape[0]
    tiles = rows // size
    route = Route(mesh_shape)
    piece_rows = route.piece_rows(size)
    count = len(piece_rows)
    piece = size // count
    per = count // 4

    for r in range(rounds):
        for p in range(count):
            at = pl.multiple_of(piece_rows[p], piece)
            start[r, pl.ds(at, piece), :] = quarters[p // per][r, pl.ds(p % per * piece, piece), :]

    for r in range(rounds):
        value = start[r].astype(jnp.float32)
        first = r * (r - 1) // 2
        for s in range(r):
            value = value - jnp.dot(among[first + s], steps[s], preferred_element_type=jnp.float32)
            value = value - jnp.where(plan[s] == plan[r], RIDGE * wide[s], 0.0)
        top = value.astype(jnp.bfloat16)
        matrix = inverse[r]
        high = matrix.astype(jnp.bfloat16)
        low = (matrix - high.astype(jnp.float32)).astype(jnp.bfloat16)
        step = jnp.dot(high, top, preferred_element_type=jnp.float32)
        step = step + jnp.dot(low, top, preferred_element_type=jnp.float32)
        wide[r] = step
        steps[r] = step.astype(jnp.bfloat16)
        for j, q in enumerate((0, 2, 1, 3)):
            for p in range(per):
                at = pl.multiple_of(piece_rows[q * per + p], piece)
                turned[r, pl.ds((j * per + p) * piece, piece), :] = steps[r, pl.ds(at, piece), :]

        begin = plan[r] * size - route.here * rows
        source = targets if r == 0 else residual
        total = jnp.zeros((8, width), jnp.float32)
        for t in range(tiles):
            where = pl.ds(t * size, size)
            part = source[where, :] - jnp.where(begin == t * size, RIDGE * wide[r], 0.0)
            for j, tall in enumerate((tall_a, tall_b)):
                rhs = turned[r, pl.ds(j * (size // 2), size // 2), :]
                part = part - jnp.dot(tall[r, where, :], rhs, preferred_element_type=jnp.float32)
            residual[where, :] = part
            total = total + jnp.sum((part * part).reshape(size // 8, 8, width), axis=0)
        folded = total[:, 0:128]
        for c in range(1, width // 128):
            folded = folded + total[:, c * 128:(c + 1) * 128]
        losses[r] = folded


def solve(mesh_shape, plan, quarters, inverse, among, tall_a, tall_b, targets):
    rounds, size, _ = inverse.shape
    rows, width = targets.shape
    return pl.pallas_call(
        functools.partial(solve_kernel, mesh_shape),
        out_shape=(
            jax.ShapeDtypeStruct((rows, width), jnp.float32),
            jax.ShapeDtypeStruct((rounds, size, width), jnp.bfloat16),
            jax.ShapeDtypeStruct((rounds, 8, 128), jnp.float32),
        ),
        in_specs=[SMEM] + [VMEM] * 9,
        out_specs=(VMEM, VMEM, VMEM),
        scratch_shapes=[
            pltpu.VMEM((rounds, size, width), jnp.bfloat16),
            pltpu.VMEM((rounds, size, width), jnp.float32),
            pltpu.VMEM((rounds, size, width), jnp.bfloat16),
        ],
        compiler_params=pltpu.CompilerParams(vmem_limit_bytes=SOLVE_VMEM),
        name="solve",
    )(plan, *quarters, inverse, among, targets, tall_a, tall_b)


def on_device(mesh_shape, points, targets, plan, block_inverse):
    rows, features = points.shape
    width = targets.shape[1]
    size = block_inverse.shape[1]
    mesh_shape = dict(mesh_shape, blocks=rows // size)
    route = Route(mesh_shape)
    total = rows * route.devices * width
    gamma = 2.0 / features
    norm_scale = -gamma * LOG2E
    inner_scale = 2.0 * gamma * LOG2E

    owner = plan * size // rows

    lead = Stream(route.spread(*pick_points(mesh_shape, plan, points, size), plan, owner))
    trail = None
    before = None
    tall_a = None
    stage = 0
    while lead.result is None:
        if stage == 1:
            held, = lead.after(targets)
            trail = Stream(route.spread(*pick_targets(mesh_shape, plan, held, size), plan, owner))
        if stage == 2:
            held, = lead.after(points)
            norms = point_norms(held, norm_scale)
        if stage == 3:
            norms, = lead.after(norms)
        if hasattr(route, "early") and tall_a is None:
            tall_a = tall_matrices(points, norms, *route.early, norm_scale, inner_scale)
            tall_a, = lead.after(tall_a)
            lead.sends, _ = lax.optimization_barrier((lead.sends, trail.sends))
        if stage == 0:
            lead.go()
        elif stage == 1:
            lead.go()
            trail.go()
        else:
            before = together(lead, trail, before)
        stage += 1
    (first_mine, last_mine), (first_other, last_other) = lead.result

    tall_b = tall_matrices(points, norms, last_mine, last_other, norm_scale, inner_scale)
    if trail.result is None:
        tall_b, = trail.after(tall_b)
        trail.go()
    ready = (first_mine, last_mine, first_other, last_other)
    among = among_matrices(mesh_shape, ready, norm_scale, inner_scale)
    while trail.result is None:
        trail.go()
    (a, b), (c, d) = trail.result
    residual, steps, partial = solve(
        mesh_shape, plan, (a, b, c, d), block_inverse, among, tall_a, tall_b, targets)
    losses = jnp.sum(route.total(partial), axis=(1, 2)) / total
    return residual, steps, losses


def solution(mesh):
    placed = (P(AXES, None), P(AXES, None), P(), P())
    return jax.shard_map(
        functools.partial(on_device, dict(mesh.shape)),
        mesh=mesh,
        in_specs=placed,
        out_specs=(P(AXES, None), P(), P()),
        check_vma=False,
    )
```

```python
import functools
import math

import jax
import jax.numpy as jnp
from jax import lax
from jax.experimental import pallas as pl
from jax.experimental.pallas import tpu as pltpu
from jax.sharding import PartitionSpec as P

RIDGE = 1.0
AXES = ("row", "col")
HALVINGS = 3
NT = (((1,), (1,)), ((), ()))
LOG2E = math.log2(math.e)
MIB = 1 << 20
SOLVE_VMEM = 16 * MIB
SMEM = pl.BlockSpec(memory_space=pltpu.SMEM)
VMEM = pl.BlockSpec(memory_space=pltpu.VMEM)
HBM = pl.BlockSpec(memory_space=pltpu.HBM)


def stage_bits(mesh_shape, late):
    cols = mesh_shape["col"].bit_length() - 1
    rows = mesh_shape["row"].bit_length() - 1
    core = cols
    along_col = list(range(cols))
    along_row = list(range(cols + 1, cols + rows))
    rest = along_col[2:] + along_row[1:]
    near, far, other = along_col[0], along_col[1], along_row[0]
    if late:
        return core, ([far, near, other] + rest, [far, other, near] + rest)
    return core, ([near, far, other] + rest, [other, near, far] + rest)


def swap(x, devices, bit_of):
    return lax.ppermute(x, AXES, [(i, i ^ (1 << bit_of(i))) for i in range(devices)])


class Route:
    def __init__(self, mesh_shape, late=False):
        self.mesh_shape = mesh_shape
        self.blocks = mesh_shape.get("blocks", 1)
        self.devices = mesh_shape["row"] * mesh_shape["col"]
        self.core, self.orders = stage_bits(mesh_shape, late)
        self.stages = len(self.orders[0])
        self.halvings = min(HALVINGS, self.stages)
        self.here = lax.axis_index("row") * mesh_shape["col"] + lax.axis_index("col")
        self.side = (self.here >> self.core) & 1

    def owner(self, block):
        return lax.div(block, self.blocks)

    def swap_core(self, x):
        return swap(x, self.devices, lambda i: self.core)

    def swap_stage(self, x, k):
        return swap(x, self.devices, lambda i: self.orders[(i >> self.core) & 1][k])

    def bit(self, index, k, side=None):
        side = self.side if side is None else side
        first, second = self.orders
        return jnp.where(side == 0, (index >> first[k]) & 1, (index >> second[k]) & 1)

    def piece_rows(self, blocksize):
        count = 1 << self.halvings
        pieces = []
        for side in (self.side, 1 - self.side):
            for p in range(count):
                row = side * (blocksize // 2)
                for k in range(self.halvings):
                    flipped = self.bit(self.here, k, side) ^ ((p >> (self.halvings - 1 - k)) & 1)
                    row = row + flipped * (blocksize >> (k + 2))
                pieces.append(row)
        return pieces

    def spread(self, send, keep, plan, owner):
        recv, = yield (self.swap_core, send),
        mine = keep
        same = ((owner >> self.core) & 1) == self.side
        for k in range(self.halvings):
            bit = self.bit(self.here, k)
            rows = mine.shape[1] // 2

            def half(which):
                return jnp.where(
                    same[:, None, None],
                    lax.dynamic_slice_in_dim(mine, which * rows, rows, 1),
                    lax.dynamic_slice_in_dim(recv, which * rows, rows, 1),
                )

            if k < 2 and mine.shape[2] > 256:
                going, staying = halve(self.mesh_shape, k, plan, mine, recv)
            else:
                going, staying = half(1 - bit), half(bit)
            recv, = yield (functools.partial(self.swap_stage, k=k), going),
            mine = staying
            same = self.bit(owner, k) == bit
        for k in range(self.halvings, self.stages):
            mine = jnp.where(same[:, None, None], mine, recv)
            recv, = yield (functools.partial(self.swap_stage, k=k), mine),
            same = self.bit(owner, k) == self.bit(self.here, k)
        mine = jnp.where(same[:, None, None], mine, recv)
        for k in reversed(range(1, self.halvings)):
            recv, = yield (functools.partial(self.swap_stage, k=k), mine),
            mine = jnp.concatenate([mine, recv], 1)
        last = functools.partial(self.swap_stage, k=0)
        recv, mine_over = yield (last, mine), (self.swap_core, mine)
        self.early = mine, mine_over
        recv_over, = yield (self.swap_core, recv),
        return (mine, recv), (mine_over, recv_over)

    def total(self, x):
        x = x + self.swap_core(x)
        for k in range(self.stages):
            x = x + swap(x, self.devices, lambda i: self.orders[0][k])
        return x


class Stream:
    def __init__(self, steps):
        self.steps = steps
        self.result = None
        self.advance(None)

    def advance(self, recv):
        try:
            pairs = self.steps.send(recv)
            self.swaps = [swap for swap, _ in pairs]
            self.sends = tuple(send for _, send in pairs)
        except StopIteration as stop:
            self.swaps = self.sends = ()
            self.result = stop.value

    def go(self):
        self.advance(tuple(swap(send) for swap, send in zip(self.swaps, self.sends)))

    def after(self, *others):
        self.sends, others = lax.optimization_barrier((self.sends, others))
        return others


def together(lead, trail, before):
    if before is not None:
        lead.sends, _ = lax.optimization_barrier((lead.sends, before))
    trail.sends, _ = lax.optimization_barrier((trail.sends, lead.sends))
    before = trail.sends
    lead.go()
    trail.go()
    return before


def block_offset(plan, r, here, rows, size):
    return pl.multiple_of(jnp.clip(plan[r] * size - here * rows, 0, rows - size), size)


def pick_points_kernel(mesh_shape, plan, points, going, staying, sems):
    slots, half, _ = going.shape
    route = Route(mesh_shape)
    copies = []
    for j, (dst, side) in enumerate(((going, 1 - route.side), (staying, route.side))):
        for r in range(slots):
            at = block_offset(plan, r, route.here, points.shape[0], 2 * half) + side * half
            src = points.at[pl.ds(pl.multiple_of(at, half), half)]
            copies.append(pltpu.make_async_copy(src, dst.at[r], sems.at[j * slots + r]))
            copies[-1].start()
    for copy in copies:
        copy.wait()


def pick_points(mesh_shape, plan, points, size):
    part = pltpu.VMEM((plan.shape[0], size // 2, points.shape[1]), points.dtype)
    return pl.pallas_call(
        functools.partial(pick_points_kernel, mesh_shape),
        out_shape=(part, part),
        in_specs=[SMEM, HBM],
        out_specs=(VMEM, VMEM),
        scratch_shapes=[pltpu.SemaphoreType.DMA((2 * plan.shape[0],))],
        name="pick_points",
    )(plan, points)


def halve_kernel(mesh_shape, k, plan, mine, recv, going, staying):
    slots, rows, _ = going.shape
    route = Route(mesh_shape)
    bit = route.bit(route.here, k)
    for r in range(slots):
        owner = route.owner(plan[r])
        if k == 0:
            same = ((owner >> route.core) & 1) == route.side
        else:
            same = route.bit(owner, k - 1) == route.bit(route.here, k - 1)
        for dst, which in ((going, 1 - bit), (staying, bit)):
            part = pl.ds(pl.multiple_of(which * rows, rows), rows)

            @pl.when(same)
            def _():
                dst[r] = mine[r, part, :]

            @pl.when(jnp.logical_not(same))
            def _():
                dst[r] = recv[r, part, :]


def halve(mesh_shape, k, plan, mine, recv):
    slots, rows, width = recv.shape
    part = jax.ShapeDtypeStruct((slots, rows // 2, width), recv.dtype)
    return pl.pallas_call(
        functools.partial(halve_kernel, mesh_shape, k),
        out_shape=(part, part),
        in_specs=[SMEM, VMEM, VMEM],
        out_specs=(VMEM, VMEM),
        compiler_params=pltpu.CompilerParams(vmem_limit_bytes=8 * MIB),
        name="halve",
    )(plan, mine, recv)


def pick_targets_kernel(mesh_shape, plan, targets, going, staying, landing, sems):
    slots, half, _ = going.shape
    route = Route(mesh_shape)
    away = pl.multiple_of((1 - route.side) * half, half)
    stay = pl.multiple_of(route.side * half, half)
    copies = []
    for r in range(slots):
        at = block_offset(plan, r, route.here, targets.shape[0], 2 * half)
        copies.append(pltpu.make_async_copy(
            targets.at[pl.ds(at, 2 * half)], landing.at[r], sems.at[r]))
        copies[-1].start()
    for r in range(slots):
        copies[r].wait()
        going[r] = landing[r, pl.ds(away, half), :].astype(going.dtype)
        staying[r] = landing[r, pl.ds(stay, half), :].astype(staying.dtype)


def pick_targets(mesh_shape, plan, targets, size):
    slots, width = plan.shape[0], targets.shape[1]
    part = pltpu.VMEM((slots, size // 2, width), jnp.bfloat16)
    return pl.pallas_call(
        functools.partial(pick_targets_kernel, mesh_shape),
        out_shape=(part, part),
        in_specs=[SMEM, HBM],
        out_specs=(VMEM, VMEM),
        scratch_shapes=[
            pltpu.VMEM((slots, size, width), targets.dtype),
            pltpu.SemaphoreType.DMA((slots,)),
        ],
        name="pick_targets",
    )(plan, targets)


def lane_sums(p, scale):
    wide = p.astype(jnp.float32)
    sums = scale * jnp.sum(wide * wide, axis=1, keepdims=True)
    return jnp.broadcast_to(sums, (p.shape[0], 128))


def norms_kernel(scale, points, norms):
    norms[...] = lane_sums(points[...], scale)


def point_norms(points, scale):
    rows, features = points.shape
    tile = rows // 2
    return pl.pallas_call(
        functools.partial(norms_kernel, scale),
        out_shape=jax.ShapeDtypeStruct((rows, 128), jnp.float32),
        grid=(rows // tile,),
        in_specs=[pl.BlockSpec((tile, features), lambda t: (t, 0))],
        out_specs=pl.BlockSpec((tile, 128), lambda t: (t, 0)),
        cost_estimate=pl.CostEstimate(flops=0, bytes_accessed=6 * MIB, transcendentals=0),
        name="norms",
    )(points)


def kernel_values(left, right, down, across, scale):
    inner = lax.dot_general(left, right, NT, preferred_element_type=jnp.float32)
    offset = jnp.concatenate([down] * (inner.shape[1] // 128), axis=1) + across
    return jnp.exp2(inner * scale + offset).astype(jnp.bfloat16)


def tall_kernel(norm_scale, scale, mine, other, points, norms, out):
    slots = mine.shape[0]
    tile = points.shape[0] // 2
    for r in range(slots):
        right = jnp.concatenate([mine[r], other[r]], axis=0)
        row = lane_sums(right, norm_scale).T[0:1, :]
        for t in range(2):
            where = pl.ds(t * tile, tile)
            out[r, where, :] = kernel_values(points[where, :], right, norms[where, :], row, scale)


def tall_matrices(points, norms, mine, other, norm_scale, scale):
    slots, quarter, features = mine.shape
    rows = points.shape[0]
    return pl.pallas_call(
        functools.partial(tall_kernel, norm_scale, scale),
        out_shape=pltpu.VMEM((slots, rows, 2 * quarter), jnp.bfloat16),
        in_specs=[VMEM] * 4,
        out_specs=VMEM,
        compiler_params=pltpu.CompilerParams(vmem_limit_bytes=12 * MIB),
        cost_estimate=pl.CostEstimate(
            flops=4 * slots * rows * quarter * features,
            bytes_accessed=8 * slots * rows * quarter,
            transcendentals=2 * slots * rows * quarter,
        ),
        name="tall",
    )(mine, other, points, norms)


def among_kernel(mesh_shape, norm_scale, scale, *refs):
    quarters = refs[0:4]
    out, blocks, down, across = refs[4:]
    rounds, size, _ = blocks.shape
    piece_rows = Route(mesh_shape).piece_rows(size)
    count = len(piece_rows)
    piece = size // count
    per = count // 4
    for r in range(rounds):
        for p in range(count):
            at = pl.multiple_of(piece_rows[p], piece)
            blocks[r, pl.ds(at, piece), :] = quarters[p // per][r, pl.ds(p % per * piece, piece), :]
        sums = lane_sums(blocks[r], norm_scale)
        down[r] = sums
        across[r] = sums.T[0:8, :]
    for s in range(rounds - 1):
        for r in range(s + 1, rounds):
            at = r * (r - 1) // 2 + s
            out[at] = kernel_values(blocks[r], blocks[s], down[r], across[s, 0:1, :], scale)


def among_matrices(mesh_shape, quarters, norm_scale, scale):
    rounds, quarter, features = quarters[0].shape
    size = 4 * quarter
    pairs = rounds * (rounds - 1) // 2
    return pl.pallas_call(
        functools.partial(among_kernel, mesh_shape, norm_scale, scale),
        out_shape=pltpu.VMEM((pairs, size, size), jnp.bfloat16),
        in_specs=[VMEM] * 4,
        out_specs=VMEM,
        scratch_shapes=[
            pltpu.VMEM((rounds, size, features), jnp.bfloat16),
            pltpu.VMEM((rounds, size, 128), jnp.float32),
            pltpu.VMEM((rounds, 8, size), jnp.float32),
        ],
        compiler_params=pltpu.CompilerParams(vmem_limit_bytes=12 * MIB),
        cost_estimate=pl.CostEstimate(
            flops=2 * pairs * size * size * features,
            bytes_accessed=4 * pairs * size * size,
            transcendentals=pairs * size * size,
        ),
        name="among",
    )(*quarters)


def solve_kernel(mesh_shape, plan, *refs):
    quarters = refs[0:4]
    inverse, among, targets, tall_a, tall_b, residual, steps, losses = refs[4:12]
    start, wide, turned = refs[12:]
    rounds, size, width = steps.shape
    rows = residual.shape[0]
    tiles = rows // size
    route = Route(mesh_shape)
    piece_rows = route.piece_rows(size)
    count = len(piece_rows)
    piece = size // count
    per = count // 4

    for r in range(rounds):
        for p in range(count):
            at = pl.multiple_of(piece_rows[p], piece)
            start[r, pl.ds(at, piece), :] = quarters[p // per][r, pl.ds(p % per * piece, piece), :]

    for r in range(rounds):
        value = start[r].astype(jnp.float32)
        first = r * (r - 1) // 2
        for s in range(r):
            value = value - jnp.dot(among[first + s], steps[s], preferred_element_type=jnp.float32)
            value = value - jnp.where(plan[s] == plan[r], RIDGE * wide[s], 0.0)
        top = value.astype(jnp.bfloat16)
        matrix = inverse[r]
        high = matrix.astype(jnp.bfloat16)
        low = (matrix - high.astype(jnp.float32)).astype(jnp.bfloat16)
        step = jnp.dot(high, top, preferred_element_type=jnp.float32)
        step = step + jnp.dot(low, top, preferred_element_type=jnp.float32)
        wide[r] = step
        steps[r] = step.astype(jnp.bfloat16)
        for j, q in enumerate((0, 2, 1, 3)):
            for p in range(per):
                at = pl.multiple_of(piece_rows[q * per + p], piece)
                turned[r, pl.ds((j * per + p) * piece, piece), :] = steps[r, pl.ds(at, piece), :]

        begin = plan[r] * size - route.here * rows
        source = targets if r == 0 else residual
        total = jnp.zeros((8, width), jnp.float32)
        for t in range(tiles):
            where = pl.ds(t * size, size)
            part = source[where, :] - jnp.where(begin == t * size, RIDGE * wide[r], 0.0)
            for j, tall in enumerate((tall_a, tall_b)):
                rhs = turned[r, pl.ds(j * (size // 2), size // 2), :]
                part = part - jnp.dot(tall[r, where, :], rhs, preferred_element_type=jnp.float32)
            residual[where, :] = part
            total = total + jnp.sum((part * part).reshape(size // 8, 8, width), axis=0)
        folded = total[:, 0:128]
        for c in range(1, width // 128):
            folded = folded + total[:, c * 128:(c + 1) * 128]
        losses[r:r + 1, :] = jnp.sum(folded, axis=0, keepdims=True)


def solve(mesh_shape, plan, quarters, inverse, among, tall_a, tall_b, targets):
    rounds, size, _ = inverse.shape
    rows, width = targets.shape
    return pl.pallas_call(
        functools.partial(solve_kernel, mesh_shape),
        out_shape=(
            jax.ShapeDtypeStruct((rows, width), jnp.float32),
            jax.ShapeDtypeStruct((rounds, size, width), jnp.bfloat16),
            jax.ShapeDtypeStruct((rounds, 128), jnp.float32),
        ),
        in_specs=[SMEM] + [VMEM] * 9,
        out_specs=(VMEM, VMEM, VMEM),
        scratch_shapes=[
            pltpu.VMEM((rounds, size, width), jnp.bfloat16),
            pltpu.VMEM((rounds, size, width), jnp.float32),
            pltpu.VMEM((rounds, size, width), jnp.bfloat16),
        ],
        compiler_params=pltpu.CompilerParams(vmem_limit_bytes=SOLVE_VMEM),
        name="solve",
    )(plan, *quarters, inverse, among, targets, tall_a, tall_b)


def on_device(mesh_shape, points, targets, plan, block_inverse):
    rows, features = points.shape
    width = targets.shape[1]
    size = block_inverse.shape[1]
    mesh_shape = dict(mesh_shape, blocks=rows // size)
    route = Route(mesh_shape)
    total = rows * route.devices * width
    gamma = 2.0 / features
    norm_scale = -gamma * LOG2E
    inner_scale = 2.0 * gamma * LOG2E

    owner = plan * size // rows

    lead = Stream(route.spread(*pick_points(mesh_shape, plan, points, size), plan, owner))
    trail = None
    before = None
    tall_a = None
    stage = 0
    while lead.result is None:
        if stage == 1:
            held, = lead.after(targets)
            trail = Stream(route.spread(*pick_targets(mesh_shape, plan, held, size), plan, owner))
        if stage == 2:
            held, = lead.after(points)
            norms = point_norms(held, norm_scale)
        if stage == 3:
            norms, = lead.after(norms)
        if hasattr(route, "early") and tall_a is None:
            tall_a = tall_matrices(points, norms, *route.early, norm_scale, inner_scale)
            tall_a, = lead.after(tall_a)
            lead.sends, _ = lax.optimization_barrier((lead.sends, trail.sends))
        if stage == 0:
            lead.go()
        elif stage == 1:
            lead.go()
            trail.go()
        else:
            before = together(lead, trail, before)
        stage += 1
    (first_mine, last_mine), (first_other, last_other) = lead.result

    tall_b = tall_matrices(points, norms, last_mine, last_other, norm_scale, inner_scale)
    if trail.result is None:
        tall_b, = trail.after(tall_b)
        trail.go()
    ready = (first_mine, last_mine, first_other, last_other)
    among = among_matrices(mesh_shape, ready, norm_scale, inner_scale)
    while trail.result is None:
        trail.go()
    (a, b), (c, d) = trail.result
    residual, steps, partial = solve(
        mesh_shape, plan, (a, b, c, d), block_inverse, among, tall_a, tall_b, targets)
    losses = jnp.sum(route.total(partial), axis=1) / total
    return residual, steps, losses


def solution(mesh):
    placed = (P(AXES, None), P(AXES, None), P(), P())
    return jax.shard_map(
        functools.partial(on_device, dict(mesh.shape)),
        mesh=mesh,
        in_specs=placed,
        out_specs=(P(AXES, None), P(), P()),
        check_vma=False,
    )
```
